256 devices in a mesh: row: 64 (over z, x_lo, y), col: 4 (over x_hi, core).
Axes of the slice: x: 4 (x_hi: 2, x_lo: 2; x = x_hi * 2 + x_lo), y: 4, z: 8, core: 2. Of those that a mesh axis runs over, the one named last changes fastest.
Arguments:
- factor_rows: float32 [2, 1024, 131072], P(None, 'col', 'row'), may hold values from -0.015625 to 0.015625
- solved_rows: float32 [131072, 512], P('row'), may hold values from -16 to 16
- right_side: float32 [2, 1024, 512], P(None, 'col', 'row'), may hold values from -6 to 6
- inverse: float32 [2, 1024, 1024], P(None, 'col'), may hold values from -1 to 2, as said below
- coupling: float32 [1024, 1024], P('col'), may hold values from -0.1875 to 0.1875
Outputs:
- forward: float32 [2, 1024, 512], P(None, 'col', 'row')
- backward: float32 [2, 1024, 512], P(None, 'col', 'row')
The draws below stay inside these ranges and needn't reach their ends.
Inputs may be any that keep to these rules, and one draw needn't show every extreme that they name: Each block of inverse is lower triangular with a positive diagonal.
All inputs are finite; a program needn't handle non-finite values.
Results may differ from the reference program's by a relative error of at most 0.00013.
Values sent between devices are 32-bit elements; how exact they have to be, the bound alone decides.
No kernel may reach another device: no remote copies, remote signals or barrier semaphores. Data moves between devices by JAX's collectives and lax.ppermute only.
A program may use at most 128 MiB of HBM per device.

```python
import math
import jax
import jax.numpy as jnp
from jax import lax

PANEL = 1024
RHS = 512
PREV = 131072


def draw_inverse(key, part):
    key = jax.random.fold_in(key, 7)
    first_key, second_key = jax.random.split(key)
    shape = (2, PANEL, PANEL)
    spread = jnp.clip(jax.random.normal(first_key, shape, jnp.float32), -4.0, 4.0)
    diagonal_values = jax.random.uniform(second_key, (2, PANEL), jnp.float32, 0.5, 1.5)
    row_index = lax.broadcasted_iota(jnp.int32, shape, 1)
    col_index = lax.broadcasted_iota(jnp.int32, shape, 2)
    lower_part = jnp.where(row_index > col_index, spread / math.sqrt(PANEL), 0.0)
    return lower_part + jnp.where(row_index == col_index, diagonal_values[:, :, None], 0.0)


def strengthened(result, stream_key, source, target, parts, factor):
    def block_of(axis_at):
        return (jnp.arange(result.shape[axis_at]) // (result.shape[axis_at] // parts)).reshape((-1,) + (1,) * (result.ndim - 1 - axis_at))

    one_side = jax.random.permutation(stream_key, parts)[block_of(target)]
    other_side = (block_of(target) + parts // 2) % parts
    return jnp.where((block_of(source) == one_side) | (block_of(source) == other_side), factor * result, result)


def block_scale(stream_key, shape, cuts, low, top_value):
    def one(dim, parts):
        heights = jax.random.uniform(jax.random.fold_in(jax.random.fold_in(stream_key, 6), dim), (parts,), jnp.float32, low / len(cuts), top_value / len(cuts))
        return jnp.repeat(jnp.exp(heights), shape[dim] // parts).reshape((-1,) + (1,) * (len(shape) - dim - 1))

    factor_of = one(*cuts[0])
    for cut in cuts[1:]:
        factor_of = factor_of * one(*cut)
    return factor_of


def scatter_about(stream_key, shape, width, bound, cuts=(), held_as=jnp.bfloat16):
    result = width * jax.random.normal(stream_key, shape, jnp.float32)
    if cuts:
        result = result * block_scale(stream_key, shape, cuts, -0.22, 0.18)
    return jnp.clip(result, -bound, bound).astype(held_as)


def bell_draw_with(key, dims, scale, most, cuts, heavy, held_as=jnp.bfloat16):
    result = scale * jax.random.normal(key, dims, jnp.float32)
    if cuts:
        result = result * block_scale(key, dims, cuts, -0.22, 0.18)
    return jnp.clip(strengthened(result, jax.random.fold_in(key, 3), *heavy), -most, most).astype(held_as)


def setup_inputs(seed: int = 0) -> dict:
    splits = jax.random.split(jax.random.key(seed), 6)
    factor_rows = scatter_about(splits[0], (2, PANEL, PREV), PREV ** -0.5, 0.015625, ((1, 4), (2, 64)), jnp.float32)
    solved_rows = bell_draw_with(splits[1], (PREV, RHS), 1.0, 16.0, ((0, 64),), (0, 1, 64, 4.0), jnp.float32)
    right_side = scatter_about(splits[2], (2, PANEL, RHS), 1.0, 6.0, ((1, 4), (2, 64)), jnp.float32)
    inverse = draw_inverse(jax.random.fold_in(splits[5], 71), 0)
    coupling = scatter_about(splits[4], (PANEL, PANEL), PANEL ** -0.5, 0.1875, ((0, 4),), jnp.float32)
    return dict(factor_rows=factor_rows, solved_rows=solved_rows, right_side=right_side, inverse=inverse, coupling=coupling)


def matmul(left, right):
    return jnp.dot(left, right, preferred_element_type=jnp.float32, precision=lax.Precision.HIGHEST)


def reference(factor_rows, solved_rows, right_side, inverse, coupling):
    flat = factor_rows.reshape(2 * PANEL, PREV)
    update = matmul(flat, solved_rows).reshape(2, PANEL, RHS)
    first_forward = matmul(inverse[0], right_side[0] - update[0])
    second_forward = matmul(inverse[1], right_side[1] - update[1] - matmul(coupling, first_forward))
    second_backward = matmul(inverse[1].T, second_forward)
    first_backward = matmul(inverse[0].T, first_forward - matmul(coupling.T, second_backward))
    forward = jnp.stack([first_forward, second_forward])
    backward = jnp.stack([first_backward, second_backward])
    return forward, backward
```

```python
import jax
import jax.numpy as jnp
from jax import lax
from jax.sharding import Mesh, PartitionSpec as P

AXES = ("z", "xl", "y", "xh", "core")
ROW = ("z", "xl", "y")
COL = ("xh", "core")


def dot(left, right, dims):
    return lax.dot_general(
        left, right, (dims, ((), ())), preferred_element_type=jnp.float32, precision=lax.Precision.HIGHEST
    )


def from_partner(block, flip):
    return lax.ppermute(block, COL, [(s, s ^ flip) for s in range(4)])


def in_order(pieces, mine):
    high, low = mine // 2, mine % 2
    a = [jnp.where(low == 1, pieces[k ^ 1], pieces[k]) for k in range(4)]
    return [jnp.where(high == 1, a[k ^ 2], a[k]) for k in range(4)]


def gather(block):
    return [block] + [from_partner(block, k) for k in (1, 2, 3)]


def total(block):
    g = gather(block)
    return (g[0] + g[1]) + (g[2] + g[3])


def block_of(array, index, axis):
    return lax.dynamic_slice_in_dim(array, index * 256, 256, axis)


def shards(factor_rows, solved_rows, right_side, inverse, coupling):
    mine = lax.axis_index(COL)
    flat = factor_rows.reshape(512, 2048)
    columns = in_order(
        [block_of(coupling, mine, 1)] + [from_partner(block_of(coupling, mine ^ k, 1), k) for k in (1, 2, 3)], mine
    )
    columns = jnp.concatenate(columns, axis=0)
    part = lax.dot_general(
        solved_rows, flat, (((0,), (1,)), ((), ())), preferred_element_type=jnp.float32, precision=lax.Precision.HIGH
    )
    part = part.reshape(8, 8, 8, 512).transpose(1, 0, 2, 3).reshape(8, 64, 512)
    part = lax.all_to_all(part, ("xl", "y"), 0, 0, tiled=True).sum(0)
    part = lax.all_to_all(part.reshape(8, 8, 512), "z", 0, 0, tiled=True).sum(0)
    right = right_side.transpose(0, 2, 1)
    r0 = right[0] - part[:, :256]
    r1 = right[1] - part[:, 256:]
    r0_whole = jnp.concatenate(in_order(gather(r0), mine), axis=1)
    f0 = dot(r0_whole, inverse[0], ((1,), (1,)))
    s_part = -dot(f0, columns, ((1,), (1,)))
    s_part = s_part + jnp.concatenate([jnp.where(mine == k, r1, 0.0) for k in range(4)], axis=1)
    f1 = dot(total(s_part), inverse[1], ((1,), (1,)))
    b1 = total(dot(f1, inverse[1], ((1,), (0,))))
    g = f0 - dot(b1, columns, ((1,), (0,)))
    b0_part = dot(g, inverse[0], ((1,), (0,)))
    got = [block_of(b0_part, mine, 1)] + [from_partner(block_of(b0_part, mine ^ k, 1), k) for k in (1, 2, 3)]
    b0 = (got[0] + got[1]) + (got[2] + got[3])
    forward = jnp.stack([f0, f1]).transpose(0, 2, 1)
    backward = jnp.stack([b0, block_of(b1, mine, 1)]).transpose(0, 2, 1)
    return (forward, backward)


def solution(mesh):
    fine = Mesh(mesh.devices.reshape(8, 2, 4, 2, 2), AXES)
    placed = (P(None, COL, ROW), P(ROW, None), P(None, COL, ROW), P(None, COL, None), P(COL, None))
    return jax.shard_map(
        shards,
        mesh=fine,
        in_specs=placed,
        out_specs=(P(None, COL, ROW), P(None, COL, ROW)),
        check_vma=False,
    )
```

```python
import jax
import jax.numpy as jnp
from jax import lax
from jax.experimental import pallas as pl
from jax.experimental.pallas import tpu as pltpu
from jax.sharding import Mesh, PartitionSpec as P

AXES = ("z", "xl", "y", "xh", "core")
ROW = ("z", "xl", "y")
COL = ("xh", "core")
NEAR = ("xl", "xh", "core")
DEPTH = 256
STEPS = 2048 // DEPTH


def split(block):
    high = block.astype(jnp.bfloat16)
    return high, (block - high.astype(jnp.float32)).astype(jnp.bfloat16)


def product_kernel(factor_hbm, solved_hbm, out_ref, factor_ref, solved_ref, sem):
    copies = []
    for k in range(STEPS):
        span = pl.ds(k * DEPTH, DEPTH)
        pair = (
            pltpu.make_async_copy(factor_hbm.at[:, span], factor_ref.at[:, span], sem.at[0, k]),
            pltpu.make_async_copy(solved_hbm.at[span, :], solved_ref.at[span, :], sem.at[1, k]),
        )
        pair[0].start()
        pair[1].start()
        copies.append(pair)
    for k in range(STEPS):
        copies[k][0].wait()
        copies[k][1].wait()
        fh, fl = split(factor_ref[:, k * DEPTH : (k + 1) * DEPTH])
        sh, sl = split(solved_ref[k * DEPTH : (k + 1) * DEPTH, :])
        term = jnp.dot(
            jnp.concatenate([fh, fh, fl], axis=1),
            jnp.concatenate([sh, sl, sh], axis=0),
            preferred_element_type=jnp.float32,
        )
        if k == 0:
            out_ref[...] = term
        else:
            out_ref[...] += term


def product(flat, solved_rows):
    return pl.pallas_call(
        product_kernel,
        in_specs=[pl.BlockSpec(memory_space=pl.ANY)] * 2,
        out_specs=pl.BlockSpec(memory_space=pltpu.VMEM),
        out_shape=pltpu.VMEM((512, 512), jnp.float32),
        scratch_shapes=[
            pltpu.VMEM((512, 2048), jnp.float32),
            pltpu.VMEM((2048, 512), jnp.float32),
            pltpu.SemaphoreType.DMA((2, STEPS)),
        ],
        compiler_params=pltpu.CompilerParams(vmem_limit_bytes=20 << 20),
        cost_estimate=pl.CostEstimate(flops=6 * 512 * 512 * 2048, bytes_accessed=9 << 20, transcendentals=0),
        name="product",
    )(pltpu.with_memory_space_constraint(flat, pltpu.HBM), pltpu.with_memory_space_constraint(solved_rows, pltpu.HBM))


def place_kernel(at_ref, update_ref, right_ref, slab_ref, out_ref, copy_ref):
    copy_ref[...] = slab_ref[...]
    turned = -update_ref[...].T
    for z in range(8):
        for p in range(8):
            out_ref[p, pl.ds(8 * z, 8), :] = turned[64 * z + 8 * p : 64 * z + 8 * p + 8, :]
    rows = pl.ds(pl.multiple_of(at_ref[1] * 8, 8), 8)
    out_ref[at_ref[0], rows, 0:256] += right_ref[0]
    out_ref[at_ref[0], rows, 256:512] += right_ref[1]


def place(at, update, right, slab):
    vmem = pl.BlockSpec(memory_space=pltpu.VMEM)
    return pl.pallas_call(
        place_kernel,
        in_specs=[pl.BlockSpec(memory_space=pltpu.SMEM), vmem, vmem, vmem],
        out_specs=[vmem, vmem],
        out_shape=[jax.ShapeDtypeStruct((8, 64, 512), jnp.float32), jax.ShapeDtypeStruct(slab.shape, jnp.float32)],
        compiler_params=pltpu.CompilerParams(vmem_limit_bytes=8 << 20),
        cost_estimate=pl.CostEstimate(flops=1 << 18, bytes_accessed=2 << 20, transcendentals=0),
        name="place",
    )(at, update, right, slab)


def sum_after(parts, awaited):
    vmem = pl.BlockSpec(memory_space=pltpu.VMEM)

    def kernel(parts_ref, *refs):
        total = parts_ref[0]
        for k in range(1, 8):
            total = total + parts_ref[k]
        refs[-1][...] = total

    return pl.pallas_call(
        kernel,
        in_specs=[vmem] + [pl.BlockSpec(memory_space=pl.ANY)] * len(awaited),
        out_specs=vmem,
        out_shape=jax.ShapeDtypeStruct(parts.shape[1:], jnp.float32),
        cost_estimate=pl.CostEstimate(flops=1 << 15, bytes_accessed=1 << 17, transcendentals=0),
        name="sum_after",
    )(parts, *awaited)


def exact(left, right, dims):
    return lax.dot_general(
        left, right, (dims, ((), ())), preferred_element_type=jnp.float32, precision=lax.Precision.HIGHEST
    )


def near(block):
    return lax.ppermute(block, "core", [(0, 1), (1, 0)])


def far(block):
    return lax.ppermute(block, NEAR, [(s, s ^ 6) for s in range(8)])


def from_col(block, flip):
    return lax.ppermute(block, COL, [(s, s ^ flip) for s in range(4)])


def from_quad(block, turn):
    pairs = []
    for z in range(8):
        for xl in range(2):
            for col in range(4):
                k = (z % 4 + turn) % 4
                step = (col - z) % 4
                step = {0: 0, 1: 1, 2: -2 if col % 2 else 2, 3: -1}[step]
                source = ((z + step) % 8 * 2 + (xl ^ (col >> 1) ^ (k >> 1))) * 4 + k
                pairs.append((source, (z * 2 + xl) * 4 + col))
    return lax.ppermute(block, ("z", "xl", "xh", "core"), pairs)


def in_order(pieces, mine):
    high, low = mine // 2, mine % 2
    a = [jnp.where(low == 1, pieces[k ^ 1], pieces[k]) for k in range(4)]
    return [jnp.where(high == 1, a[k ^ 2], a[k]) for k in range(4)]


def turned(pieces, quad):
    a = [jnp.where(quad % 2 == 1, pieces[k - 1], pieces[k]) for k in range(4)]
    return [jnp.where(quad // 2 == 1, a[k - 2], a[k]) for k in range(4)]


def block_of(array, index):
    return lax.dynamic_slice_in_dim(array, index * 256, 256, 1)


def added(blocks):
    return (blocks[0] + blocks[1]) + (blocks[2] + blocks[3])


def shards(factor_rows, solved_rows, right_side, inverse, coupling):
    mine = lax.axis_index(COL)
    quad = lax.axis_index("z") % 4
    at = jnp.stack([lax.axis_index(("xl", "y")), lax.axis_index("z")])

    slab = lax.dynamic_slice(inverse, (0, 0, quad * 256), (1, 256, 256))[0]
    slab_far = far(slab)
    update = product(factor_rows.reshape(512, 2048), solved_rows)
    part, slab_far = place(at, update, right_side.transpose(0, 2, 1), slab_far)
    part = lax.all_to_all(part, ("xl", "y"), 0, 0, tiled=True)
    whole = jnp.concatenate(in_order([slab, near(slab), slab_far, near(slab_far)], mine), axis=0)
    middle = exact(coupling, whole, ((1,), (0,)))
    part = sum_after(part, [middle])
    columns = [from_quad(middle, k) for k in range(4)]
    part = lax.all_to_all(part.reshape(8, 8, 512), "z", 0, 0, tiled=True)
    r = sum_after(part, columns)
    columns = jnp.concatenate(turned(columns, quad), axis=0)

    r0, r1 = r[:, :256], r[:, 256:]
    s = jnp.concatenate([jnp.where(mine == k, r1, 0.0) for k in range(4)], axis=1) - exact(r0, columns, ((1,), (1,)))
    sent = jnp.concatenate([r0, s], axis=1)
    got = [sent] + [from_col(sent, k) for k in (1, 2, 3)]
    f0 = exact(jnp.concatenate(in_order([g[:, :256] for g in got], mine), axis=1), inverse[0], ((1,), (1,)))
    f1 = exact(added([g[:, 256:] for g in got]), inverse[1], ((1,), (1,)))
    b0 = exact(f0, inverse[0], ((1,), (0,)))
    b1 = exact(f1, inverse[1], ((1,), (0,)))
    sent = [jnp.concatenate([block_of(b0, mine ^ k), b1], axis=1) for k in range(4)]
    got = [sent[0]] + [from_col(sent[k], k) for k in (1, 2, 3)]
    b = added(got)
    b1 = b[:, 256:]
    b0 = b[:, :256] - exact(b1, columns, ((1,), (0,)))
    forward = jnp.stack([f0, f1])
    backward = jnp.stack([b0, block_of(b1, mine)])
    return (forward.transpose(0, 2, 1), backward.transpose(0, 2, 1))


def solution(mesh):
    fine = Mesh(mesh.devices.reshape(8, 2, 4, 2, 2), AXES)
    placed = (P(None, COL, ROW), P(ROW, None), P(None, COL, ROW), P(None, COL, None), P(COL, None))
    return jax.shard_map(
        shards,
        mesh=fine,
        in_specs=placed,
        out_specs=(P(None, COL, ROW), P(None, COL, ROW)),
        check_vma=False,
    )
```

```python
import jax
import jax.numpy as jnp
from jax import lax
from jax.experimental import pallas as pl
from jax.experimental.pallas import tpu as pltpu
from jax.sharding import Mesh, PartitionSpec as P

AXES = ("z", "xl", "y", "xh", "core")
ROW = ("z", "xl", "y")
COL = ("xh", "core")
NEAR = ("xl", "xh", "core")
DEPTH = 256
STEPS = 2048 // DEPTH


def split(block):
    high = block.astype(jnp.bfloat16)
    return high, (block - high.astype(jnp.float32)).astype(jnp.bfloat16)


def product_kernel(at_ref, factor_hbm, solved_hbm, inverse_hbm, out_ref, slab_ref, factor_ref, solved_ref, sem, slab_sem):
    span = pl.ds(pl.multiple_of(at_ref[2] * 256, 256), 256)
    slab = pltpu.make_async_copy(inverse_hbm.at[0, :, span], slab_ref, slab_sem)
    copies = []
    for k in range(STEPS):
        span = pl.ds(k * DEPTH, DEPTH)
        pair = (
            pltpu.make_async_copy(factor_hbm.at[:, span], factor_ref.at[:, span], sem.at[0, k]),
            pltpu.make_async_copy(solved_hbm.at[span, :], solved_ref.at[span, :], sem.at[1, k]),
        )
        pair[0].start()
        pair[1].start()
        copies.append(pair)
    for k in range(STEPS):
        copies[k][0].wait()
        copies[k][1].wait()
        fh, fl = split(factor_ref[:, k * DEPTH : (k + 1) * DEPTH])
        sh, sl = split(solved_ref[k * DEPTH : (k + 1) * DEPTH, :])
        term = jnp.dot(
            jnp.concatenate([fh, fh, fl], axis=1),
            jnp.concatenate([sh, sl, sh], axis=0),
            preferred_element_type=jnp.float32,
        )
        if k == 0:
            slab.start()
            out_ref[...] = term
        else:
            out_ref[...] += term
    slab.wait()


def product(at, flat, solved_rows, inverse):
    return pl.pallas_call(
        product_kernel,
        in_specs=[pl.BlockSpec(memory_space=pltpu.SMEM)] + [pl.BlockSpec(memory_space=pl.ANY)] * 3,
        out_specs=[pl.BlockSpec(memory_space=pltpu.VMEM)] * 2,
        out_shape=[pltpu.VMEM((512, 512), jnp.float32), jax.ShapeDtypeStruct((256, 256), jnp.float32)],
        scratch_shapes=[
            pltpu.VMEM((512, 2048), jnp.float32),
            pltpu.VMEM((2048, 512), jnp.float32),
            pltpu.SemaphoreType.DMA((2, STEPS)),
            pltpu.SemaphoreType.DMA,
        ],
        compiler_params=pltpu.CompilerParams(vmem_limit_bytes=20 << 20),
        cost_estimate=pl.CostEstimate(flops=6 * 512 * 512 * 2048, bytes_accessed=9 << 20, transcendentals=0),
        name="product",
    )(at, *(pltpu.with_memory_space_constraint(x, pltpu.HBM) for x in (flat, solved_rows, inverse)))


def place_kernel(at_ref, update_ref, right_ref, out_ref):
    turned = -update_ref[...].T
    for z in range(8):
        for p in range(8):
            out_ref[p, pl.ds(8 * z, 8), :] = turned[64 * z + 8 * p : 64 * z + 8 * p + 8, :]
    rows = pl.ds(pl.multiple_of(at_ref[1] * 8, 8), 8)
    out_ref[at_ref[0], rows, 0:256] += right_ref[0]
    out_ref[at_ref[0], rows, 256:512] += right_ref[1]


def place(at, update, right):
    vmem = pl.BlockSpec(memory_space=pltpu.VMEM)
    return pl.pallas_call(
        place_kernel,
        in_specs=[pl.BlockSpec(memory_space=pltpu.SMEM), vmem, vmem],
        out_specs=vmem,
        out_shape=jax.ShapeDtypeStruct((8, 64, 512), jnp.float32),
        compiler_params=pltpu.CompilerParams(vmem_limit_bytes=8 << 20),
        cost_estimate=pl.CostEstimate(flops=1 << 18, bytes_accessed=2 << 20, transcendentals=0),
        name="place",
    )(at, update, right)


def sum_kernel(parts_ref, out_ref):
    total = parts_ref[0]
    for k in range(1, 8):
        total = total + parts_ref[k]
    out_ref[...] = total


def sum_parts(parts):
    vmem = pl.BlockSpec(memory_space=pltpu.VMEM)
    return pl.pallas_call(
        sum_kernel,
        in_specs=[vmem],
        out_specs=vmem,
        out_shape=jax.ShapeDtypeStruct(parts.shape[1:], jnp.float32),
        compiler_params=pltpu.CompilerParams(vmem_limit_bytes=8 << 20),
        cost_estimate=pl.CostEstimate(flops=1 << 18, bytes_accessed=1 << 20, transcendentals=0),
        name="sum_parts",
    )(parts)


def after(block, awaited):
    return lax.optimization_barrier((block, awaited))[0]


def exact(left, right, dims):
    return lax.dot_general(
        left, right, (dims, ((), ())), preferred_element_type=jnp.float32, precision=lax.Precision.HIGHEST
    )


def block_product(at, left, pieces, name):
    vmem = pl.BlockSpec(memory_space=pltpu.VMEM)

    def kernel(at_ref, left_ref, p0, p1, p2, p3, out_ref, whole_ref):
        for flip, piece in enumerate((p0, p1, p2, p3)):
            whole_ref[pl.ds(pl.multiple_of((at_ref[3] ^ flip) * 256, 256), 256), :] = piece[...]
        out_ref[...] = exact(left_ref[...], whole_ref[...], ((1,), (0,)))

    return pl.pallas_call(
        kernel,
        in_specs=[pl.BlockSpec(memory_space=pltpu.SMEM)] + [vmem] * 5,
        out_specs=vmem,
        out_shape=jax.ShapeDtypeStruct((256, 256), jnp.float32),
        scratch_shapes=[pltpu.VMEM((1024, 256), jnp.float32)],
        compiler_params=pltpu.CompilerParams(vmem_limit_bytes=16 << 20),
        cost_estimate=pl.CostEstimate(flops=1 << 10, bytes_accessed=1 << 10, transcendentals=0),
        name=name,
    )(at, left, *pieces)


def near(block):
    return lax.ppermute(block, "core", [(0, 1), (1, 0)])


def far(block):
    return lax.ppermute(block, NEAR, [(s, s ^ 6) for s in range(8)])


def from_col(block, flip):
    return lax.ppermute(block, COL, [(s, s ^ flip) for s in range(4)])


def from_quad(block, turn):
    pairs = []
    for z in range(8):
        for xl in range(2):
            for col in range(4):
                k = (z % 4 + turn) % 4
                step = (col - z) % 4
                step = {0: 0, 1: 1, 2: -2 if col % 2 else 2, 3: -1}[step]
                source = ((z + step) % 8 * 2 + (xl ^ (col >> 1) ^ (k >> 1))) * 4 + k
                pairs.append((source, (z * 2 + xl) * 4 + col))
    return lax.ppermute(block, ("z", "xl", "xh", "core"), pairs)


def in_order(pieces, mine):
    high, low = mine // 2, mine % 2
    a = [jnp.where(low == 1, pieces[k ^ 1], pieces[k]) for k in range(4)]
    return [jnp.where(high == 1, a[k ^ 2], a[k]) for k in range(4)]


def turned(pieces, quad):
    a = [jnp.where(quad % 2 == 1, pieces[k - 1], pieces[k]) for k in range(4)]
    return [jnp.where(quad // 2 == 1, a[k - 2], a[k]) for k in range(4)]


def block_of(array, index):
    return lax.dynamic_slice_in_dim(array, index * 256, 256, 1)


def added(blocks):
    return (blocks[0] + blocks[1]) + (blocks[2] + blocks[3])


def shards(factor_rows, solved_rows, right_side, inverse, coupling):
    mine = lax.axis_index(COL)
    quad = lax.axis_index("z") % 4
    at = jnp.stack([lax.axis_index(("xl", "y")), lax.axis_index("z"), quad, mine])

    update, slab = product(at, factor_rows.reshape(512, 2048), solved_rows, inverse)
    slab_far = far(slab)
    part = place(at, update, right_side.transpose(0, 2, 1))
    slab_far = after(slab_far, part)
    part = lax.all_to_all(part, ("xl", "y"), 0, 0, tiled=True)
    beyond = jnp.concatenate([near(slab_far[64 * k : 64 * k + 64]) for k in range(4)], axis=0)
    middle = block_product(at, coupling, [slab, near(slab), slab_far, beyond], "middle")
    part = after(sum_parts(part), middle)
    columns = [from_quad(middle, k) for k in range(4)]
    part = lax.all_to_all(part.reshape(8, 8, 512), "z", 0, 0, tiled=True)
    r = after(part.sum(0), columns)
    columns = turned(columns, quad)
    rows = jnp.concatenate([c.T for c in columns], axis=1)
    columns = jnp.concatenate(columns, axis=0)

    r0, r1 = r[:, :256], r[:, 256:]
    s = jnp.concatenate([jnp.where(mine == k, r1, 0.0) for k in range(4)], axis=1) - exact(r0, rows, ((1,), (0,)))
    sent = jnp.concatenate([r0, s], axis=1)
    got = [sent] + [from_col(sent, k) for k in (1, 2, 3)]
    f0 = exact(jnp.concatenate(in_order([g[:, :256] for g in got], mine), axis=1), inverse[0], ((1,), (1,)))
    f1 = exact(added([g[:, 256:] for g in got]), inverse[1], ((1,), (1,)))
    b0 = exact(f0, inverse[0], ((1,), (0,)))
    b1 = exact(f1, inverse[1], ((1,), (0,)))
    sent = [jnp.concatenate([block_of(b0, mine ^ k), b1], axis=1) for k in range(4)]
    got = [sent[0]] + [from_col(sent[k], k) for k in (1, 2, 3)]
    b = added(got)
    b1 = b[:, 256:]
    b0 = b[:, :256] - exact(b1, columns, ((1,), (0,)))
    forward = jnp.stack([f0, f1])
    backward = jnp.stack([b0, block_of(b1, mine)])
    return (forward.transpose(0, 2, 1), backward.transpose(0, 2, 1))


def solution(mesh):
    fine = Mesh(mesh.devices.reshape(8, 2, 4, 2, 2), AXES)
    placed = (P(None, COL, ROW), P(ROW, None), P(None, COL, ROW), P(None, COL, None), P(COL, None))
    return jax.shard_map(
        shards,
        mesh=fine,
        in_specs=placed,
        out_specs=(P(None, COL, ROW), P(None, COL, ROW)),
        check_vma=False,
    )
```

```python
import jax
import jax.numpy as jnp
from jax import lax
from jax.experimental import pallas as pl
from jax.experimental.pallas import tpu as pltpu
from jax.sharding import Mesh, PartitionSpec as P

AXES = ("z", "xl", "y", "xh", "core")
ROW = ("z", "xl", "y")
COL = ("xh", "core")
NEAR = ("xl", "xh", "core")
DEPTH = 256
STEPS = 2048 // DEPTH


def split(block):
    high = block.astype(jnp.bfloat16)
    return high, (block - high.astype(jnp.float32)).astype(jnp.bfloat16)


def product_kernel(at_ref, factor_hbm, solved_hbm, inverse_hbm, out_ref, slab_ref, factor_ref, solved_ref, sem, slab_sem):
    span = pl.ds(pl.multiple_of(at_ref[2] * 256, 256), 256)
    slab = pltpu.make_async_copy(inverse_hbm.at[0, :, span], slab_ref, slab_sem)
    copies = []
    for k in range(STEPS):
        span = pl.ds(k * DEPTH, DEPTH)
        pair = (
            pltpu.make_async_copy(factor_hbm.at[:, span], factor_ref.at[:, span], sem.at[0, k]),
            pltpu.make_async_copy(solved_hbm.at[span, :], solved_ref.at[span, :], sem.at[1, k]),
        )
        pair[0].start()
        pair[1].start()
        copies.append(pair)
    for k in range(STEPS):
        copies[k][0].wait()
        copies[k][1].wait()
        fh, fl = split(factor_ref[:, k * DEPTH : (k + 1) * DEPTH])
        sh, sl = split(solved_ref[k * DEPTH : (k + 1) * DEPTH, :])
        term = jnp.dot(
            jnp.concatenate([fh, fh, fl], axis=1),
            jnp.concatenate([sh, sl, sh], axis=0),
            preferred_element_type=jnp.float32,
        )
        if k == 0:
            slab.start()
            out_ref[...] = term
        else:
            out_ref[...] += term
    slab.wait()


def product(at, flat, solved_rows, inverse):
    return pl.pallas_call(
        product_kernel,
        in_specs=[pl.BlockSpec(memory_space=pltpu.SMEM)] + [pl.BlockSpec(memory_space=pl.ANY)] * 3,
        out_specs=[pl.BlockSpec(memory_space=pltpu.VMEM)] * 2,
        out_shape=[pltpu.VMEM((512, 512), jnp.float32), jax.ShapeDtypeStruct((256, 256), jnp.float32)],
        scratch_shapes=[
            pltpu.VMEM((512, 2048), jnp.float32),
            pltpu.VMEM((2048, 512), jnp.float32),
            pltpu.SemaphoreType.DMA((2, STEPS)),
            pltpu.SemaphoreType.DMA,
        ],
        compiler_params=pltpu.CompilerParams(vmem_limit_bytes=20 << 20),
        cost_estimate=pl.CostEstimate(flops=6 * 512 * 512 * 2048, bytes_accessed=9 << 20, transcendentals=0),
        name="product",
    )(at, *(pltpu.with_memory_space_constraint(x, pltpu.HBM) for x in (flat, solved_rows, inverse)))


def place_kernel(at_ref, update_ref, right_ref, out_ref):
    turned = -update_ref[...].T
    for z in range(8):
        for p in range(8):
            out_ref[p, pl.ds(8 * z, 8), :] = turned[64 * z + 8 * p : 64 * z + 8 * p + 8, :]
    rows = pl.ds(pl.multiple_of(at_ref[1] * 8, 8), 8)
    out_ref[at_ref[0], rows, 0:256] += right_ref[0]
    out_ref[at_ref[0], rows, 256:512] += right_ref[1]


def place(at, update, right):
    vmem = pl.BlockSpec(memory_space=pltpu.VMEM)
    return pl.pallas_call(
        place_kernel,
        in_specs=[pl.BlockSpec(memory_space=pltpu.SMEM), vmem, vmem],
        out_specs=vmem,
        out_shape=jax.ShapeDtypeStruct((8, 64, 512), jnp.float32),
        compiler_params=pltpu.CompilerParams(vmem_limit_bytes=8 << 20),
        cost_estimate=pl.CostEstimate(flops=1 << 18, bytes_accessed=2 << 20, transcendentals=0),
        name="place",
    )(at, update, right)


def sum_kernel(parts_ref, out_ref):
    total = parts_ref[0]
    for k in range(1, 8):
        total = total + parts_ref[k]
    out_ref[...] = total


def sum_parts(parts):
    vmem = pl.BlockSpec(memory_space=pltpu.VMEM)
    return pl.pallas_call(
        sum_kernel,
        in_specs=[vmem],
        out_specs=vmem,
        out_shape=jax.ShapeDtypeStruct(parts.shape[1:], jnp.float32),
        compiler_params=pltpu.CompilerParams(vmem_limit_bytes=8 << 20),
        cost_estimate=pl.CostEstimate(flops=1 << 18, bytes_accessed=1 << 20, transcendentals=0),
        name="sum_parts",
    )(parts)


def after(block, awaited):
    return lax.optimization_barrier((block, awaited))[0]


def exact(left, right, dims):
    return lax.dot_general(
        left, right, (dims, ((), ())), preferred_element_type=jnp.float32, precision=lax.Precision.HIGHEST
    )


def block_product(at, left, pieces, name):
    vmem = pl.BlockSpec(memory_space=pltpu.VMEM)

    def kernel(at_ref, left_ref, p0, p1, p2, p3, out_ref, whole_ref):
        for flip, piece in enumerate((p0, p1, p2, p3)):
            whole_ref[pl.ds(pl.multiple_of((at_ref[3] ^ flip) * 256, 256), 256), :] = piece[...]
        out_ref[...] = exact(left_ref[...], whole_ref[...], ((1,), (0,)))

    return pl.pallas_call(
        kernel,
        in_specs=[pl.BlockSpec(memory_space=pltpu.SMEM)] + [vmem] * 5,
        out_specs=vmem,
        out_shape=jax.ShapeDtypeStruct((256, 256), jnp.float32),
        scratch_shapes=[pltpu.VMEM((1024, 256), jnp.float32)],
        compiler_params=pltpu.CompilerParams(vmem_limit_bytes=16 << 20),
        cost_estimate=pl.CostEstimate(flops=1 << 10, bytes_accessed=1 << 10, transcendentals=0),
        name=name,
    )(at, left, *pieces)


def near(block):
    return lax.ppermute(block, "core", [(0, 1), (1, 0)])


def far(block):
    return lax.ppermute(block, NEAR, [(s, s ^ 6) for s in range(8)])


def opposite(block):
    return lax.ppermute(block, "xh", [(0, 1), (1, 0)])


def ordered(second, here, there):
    return jnp.concatenate([jnp.where(second == 1, there, here), jnp.where(second == 1, here, there)], axis=1)


def from_quad(block, turn):
    pairs = []
    for z in range(8):
        for xl in range(2):
            for col in range(4):
                k = (z % 4 + turn) % 4
                step = (col - z) % 4
                step = {0: 0, 1: 1, 2: -2 if col % 2 else 2, 3: -1}[step]
                source = ((z + step) % 8 * 2 + (xl ^ (col >> 1) ^ (k >> 1))) * 4 + k
                pairs.append((source, (z * 2 + xl) * 4 + col))
    return lax.ppermute(block, ("z", "xl", "xh", "core"), pairs)


def in_order(pieces, mine):
    high, low = mine // 2, mine % 2
    a = [jnp.where(low == 1, pieces[k ^ 1], pieces[k]) for k in range(4)]
    return [jnp.where(high == 1, a[k ^ 2], a[k]) for k in range(4)]


def turned(pieces, quad):
    a = [jnp.where(quad % 2 == 1, pieces[k - 1], pieces[k]) for k in range(4)]
    return [jnp.where(quad // 2 == 1, a[k - 2], a[k]) for k in range(4)]


def block_of(array, index):
    return lax.dynamic_slice_in_dim(array, index * 256, 256, 1)


def shards(factor_rows, solved_rows, right_side, inverse, coupling):
    mine = lax.axis_index(COL)
    quad = lax.axis_index("z") % 4
    at = jnp.stack([lax.axis_index(("xl", "y")), lax.axis_index("z"), quad, mine])

    update, slab = product(at, factor_rows.reshape(512, 2048), solved_rows, inverse)
    slab_far = far(slab)
    part = place(at, update, right_side.transpose(0, 2, 1))
    slab_far = after(slab_far, part)
    part = lax.all_to_all(part, ("xl", "y"), 0, 0, tiled=True)
    beyond = jnp.concatenate([near(slab_far[64 * k : 64 * k + 64]) for k in range(4)], axis=0)
    middle = block_product(at, coupling, [slab, near(slab), slab_far, beyond], "middle")
    part = after(sum_parts(part), middle)
    columns = [from_quad(middle, k) for k in range(4)]
    part = lax.all_to_all(part.reshape(8, 8, 512), "z", 0, 0, tiled=True)
    r = part.sum(0)
    columns = turned(columns, quad)
    rows = jnp.concatenate([c.T for c in columns], axis=1)
    columns = jnp.concatenate(columns, axis=0)

    r0, r1 = r[:, :256], r[:, 256:]
    s = jnp.concatenate([jnp.where(mine == k, r1, 0.0) for k in range(4)], axis=1) - exact(r0, rows, ((1,), (0,)))
    core, xh = lax.axis_index("core"), lax.axis_index("xh")
    sent = jnp.concatenate([r0, s], axis=1)
    other = near(sent)
    pair = ordered(core, sent[:, :256], other[:, :256])
    sent = jnp.concatenate([pair, sent[:, 256:] + other[:, 256:]], axis=1)
    other = opposite(sent)
    f0 = exact(ordered(xh, sent[:, :512], other[:, :512]), inverse[0], ((1,), (1,)))
    f1 = exact(sent[:, 512:] + other[:, 512:], inverse[1], ((1,), (1,)))
    b0 = exact(f0, inverse[0], ((1,), (0,)))
    b1 = exact(f1, inverse[1], ((1,), (0,)))
    other = near(jnp.concatenate([b1, block_of(b0, mine ^ 1), block_of(b0, mine ^ 3)], axis=1))
    sums = jnp.concatenate([b1, block_of(b0, mine), block_of(b0, mine ^ 2)], axis=1) + other
    other = opposite(jnp.concatenate([sums[:, :1024], sums[:, 1280:]], axis=1))
    b = sums[:, :1280] + other
    b1 = b[:, :1024]
    b0 = b[:, 1024:] - exact(b1, columns, ((1,), (0,)))
    forward = jnp.stack([f0, f1])
    backward = jnp.stack([b0, block_of(b1, mine)])
    return (forward.transpose(0, 2, 1), backward.transpose(0, 2, 1))


def solution(mesh):
    fine = Mesh(mesh.devices.reshape(8, 2, 4, 2, 2), AXES)
    placed = (P(None, COL, ROW), P(ROW, None), P(None, COL, ROW), P(None, COL, None), P(COL, None))
    return jax.shard_map(
        shards,
        mesh=fine,
        in_specs=placed,
        out_specs=(P(None, COL, ROW), P(None, COL, ROW)),
        check_vma=False,
    )
```

```python
import jax
import jax.numpy as jnp
from jax import lax
from jax.experimental import pallas as pl
from jax.experimental.pallas import tpu as pltpu
from jax.sharding import Mesh, PartitionSpec as P

AXES = ("z", "xl", "y", "xh", "core")
ROW = ("z", "xl", "y")
COL = ("xh", "core")
NEAR = ("xl", "xh", "core")
DEPTH = 256
STEPS = 2048 // DEPTH


def split(block):
    high = block.astype(jnp.bfloat16)
    return high, (block - high.astype(jnp.float32)).astype(jnp.bfloat16)


def product_kernel(at_ref, factor_hbm, solved_hbm, inverse_hbm, out_ref, slab_ref, factor_ref, solved_ref, sem, slab_sem):
    span = pl.ds(pl.multiple_of(at_ref[2] * 256, 256), 256)
    slab = pltpu.make_async_copy(inverse_hbm.at[0, :, span], slab_ref, slab_sem)
    copies = []
    for k in range(STEPS):
        span = pl.ds(k * DEPTH, DEPTH)
        pair = (
            pltpu.make_async_copy(factor_hbm.at[:, span], factor_ref.at[:, span], sem.at[0, k]),
            pltpu.make_async_copy(solved_hbm.at[span, :], solved_ref.at[span, :], sem.at[1, k]),
        )
        pair[0].start()
        pair[1].start()
        copies.append(pair)
    for first, count in ((0, 2), (2, 2), (4, 2), (6, 1), (7, 1)):
        for k in range(first, first + count):
            copies[k][0].wait()
            copies[k][1].wait()
        fh, fl = split(factor_ref[:, first * DEPTH : (first + count) * DEPTH])
        sh, sl = split(solved_ref[first * DEPTH : (first + count) * DEPTH, :])
        term = jnp.dot(
            jnp.concatenate([fh, fh, fl], axis=1),
            jnp.concatenate([sh, sl, sh], axis=0),
            preferred_element_type=jnp.float32,
        )
        if first == 0:
            slab.start()
            out_ref[...] = term
        else:
            out_ref[...] += term
    slab.wait()


def product(at, flat, solved_rows, inverse):
    return pl.pallas_call(
        product_kernel,
        in_specs=[pl.BlockSpec(memory_space=pltpu.SMEM)] + [pl.BlockSpec(memory_space=pl.ANY)] * 3,
        out_specs=[pl.BlockSpec(memory_space=pltpu.VMEM)] * 2,
        out_shape=[pltpu.VMEM((512, 512), jnp.float32), jax.ShapeDtypeStruct((256, 256), jnp.float32)],
        scratch_shapes=[
            pltpu.VMEM((512, 2048), jnp.float32),
            pltpu.VMEM((2048, 512), jnp.float32),
            pltpu.SemaphoreType.DMA((2, STEPS)),
            pltpu.SemaphoreType.DMA,
        ],
        compiler_params=pltpu.CompilerParams(vmem_limit_bytes=20 << 20),
        cost_estimate=pl.CostEstimate(flops=6 * 512 * 512 * 2048, bytes_accessed=9 << 20, transcendentals=0),
        name="product",
    )(at, *(pltpu.with_memory_space_constraint(x, pltpu.HBM) for x in (flat, solved_rows, inverse)))


def place_kernel(at_ref, update_ref, right_ref, out_hbm, out_ref, sem):
    copies = []
    for part in range(4):
        turned = -update_ref[:, 128 * part : 128 * part + 128].T
        for half in range(2):
            rows = slice(16 * part + 8 * half, 16 * part + 8 * half + 8)
            for p in range(8):
                out_ref[p, rows, :] = turned[64 * half + 8 * p : 64 * half + 8 * p + 8, :]

        @pl.when(at_ref[1] // 2 == part)
        def _():
            rows = pl.ds(pl.multiple_of(at_ref[1] * 8, 8), 8)
            out_ref[at_ref[0], rows, 0:256] += right_ref[0]
            out_ref[at_ref[0], rows, 256:512] += right_ref[1]

        rows = pl.ds(16 * part, 16)
        copies.append(pltpu.make_async_copy(out_ref.at[:, rows, :], out_hbm.at[:, rows, :], sem.at[part]))
        copies[-1].start()
    for copy in copies:
        copy.wait()


def place(at, update, right):
    vmem = pl.BlockSpec(memory_space=pltpu.VMEM)
    return pl.pallas_call(
        place_kernel,
        in_specs=[pl.BlockSpec(memory_space=pltpu.SMEM), vmem, vmem],
        out_specs=pl.BlockSpec(memory_space=pl.ANY),
        out_shape=jax.ShapeDtypeStruct((8, 64, 512), jnp.float32),
        scratch_shapes=[pltpu.VMEM((8, 64, 512), jnp.float32), pltpu.SemaphoreType.DMA((4,))],
        compiler_params=pltpu.CompilerParams(vmem_limit_bytes=8 << 20),
        cost_estimate=pl.CostEstimate(flops=1 << 18, bytes_accessed=2 << 20, transcendentals=0),
        name="place",
    )(at, update, right)


def sum_kernel(parts_ref, out_ref):
    total = parts_ref[0]
    for k in range(1, 8):
        total = total + parts_ref[k]
    out_ref[...] = total


def sum_parts(parts):
    vmem = pl.BlockSpec(memory_space=pltpu.VMEM)
    return pl.pallas_call(
        sum_kernel,
        in_specs=[vmem],
        out_specs=vmem,
        out_shape=jax.ShapeDtypeStruct(parts.shape[1:], jnp.float32),
        compiler_params=pltpu.CompilerParams(vmem_limit_bytes=8 << 20),
        cost_estimate=pl.CostEstimate(flops=1 << 18, bytes_accessed=1 << 20, transcendentals=0),
        name="sum_parts",
    )(parts)


def after(block, awaited):
    return lax.optimization_barrier((block, awaited))[0]


def exact(left, right, dims):
    return lax.dot_general(
        left, right, (dims, ((), ())), preferred_element_type=jnp.float32, precision=lax.Precision.HIGH
    )


def block_product(at, left, pieces, name):
    vmem = pl.BlockSpec(memory_space=pltpu.VMEM)

    def kernel(at_ref, left_ref, p0, p1, p2, p3, out_ref, whole_ref):
        for flip, piece in enumerate((p0, p1, p2, p3)):
            whole_ref[pl.ds(pl.multiple_of((at_ref[3] ^ flip) * 256, 256), 256), :] = piece[...]
        ah, al = split(left_ref[...])
        bh, bl = split(whole_ref[...])
        out_ref[...] = jnp.dot(
            jnp.concatenate([ah, ah, al], axis=1),
            jnp.concatenate([bh, bl, bh], axis=0),
            preferred_element_type=jnp.float32,
        )

    return pl.pallas_call(
        kernel,
        in_specs=[pl.BlockSpec(memory_space=pltpu.SMEM)] + [vmem] * 5,
        out_specs=vmem,
        out_shape=jax.ShapeDtypeStruct((256, 256), jnp.float32),
        scratch_shapes=[pltpu.VMEM((1024, 256), jnp.float32)],
        compiler_params=pltpu.CompilerParams(vmem_limit_bytes=16 << 20),
        cost_estimate=pl.CostEstimate(flops=1 << 10, bytes_accessed=1 << 10, transcendentals=0),
        name=name,
    )(at, left, *pieces)


def near(block):
    return lax.ppermute(block, "core", [(0, 1), (1, 0)])


def far(block):
    return lax.ppermute(block, NEAR, [(s, s ^ 6) for s in range(8)])


def opposite(block):
    return lax.ppermute(block, "xh", [(0, 1), (1, 0)])


def ordered(second, here, there):
    return jnp.concatenate([jnp.where(second == 1, there, here), jnp.where(second == 1, here, there)], axis=1)


def from_quad(block, turn):
    pairs = []
    for z in range(8):
        for xl in range(2):
            for col in range(4):
                k = (z % 4 + turn) % 4
                step = (col - z) % 4
                step = {0: 0, 1: 1, 2: -2 if col % 2 else 2, 3: -1}[step]
                source = ((z + step) % 8 * 2 + (xl ^ (col >> 1) ^ (k >> 1))) * 4 + k
                pairs.append((source, (z * 2 + xl) * 4 + col))
    return lax.ppermute(block, ("z", "xl", "xh", "core"), pairs)


def in_order(pieces, mine):
    high, low = mine // 2, mine % 2
    a = [jnp.where(low == 1, pieces[k ^ 1], pieces[k]) for k in range(4)]
    return [jnp.where(high == 1, a[k ^ 2], a[k]) for k in range(4)]


def turned(pieces, quad):
    a = [jnp.where(quad % 2 == 1, pieces[k - 1], pieces[k]) for k in range(4)]
    return [jnp.where(quad // 2 == 1, a[k - 2], a[k]) for k in range(4)]


def block_of(array, index):
    return lax.dynamic_slice_in_dim(array, index * 256, 256, 1)


def shards(factor_rows, solved_rows, right_side, inverse, coupling):
    mine = lax.axis_index(COL)
    quad = lax.axis_index("z") % 4
    at = jnp.stack([lax.axis_index(("xl", "y")), lax.axis_index("z"), quad, mine])

    update, slab = product(at, factor_rows.reshape(512, 2048), solved_rows, inverse)
    slab_far = far(slab)
    part = place(at, update, right_side.transpose(0, 2, 1))
    slab_far = after(slab_far, part)
    part = lax.all_to_all(part, ("xl", "y"), 0, 0, tiled=True)
    beyond = jnp.concatenate([near(slab_far[64 * k : 64 * k + 64]) for k in range(4)], axis=0)
    middle = block_product(at, coupling, [slab, near(slab), slab_far, beyond], "middle")
    part = after(sum_parts(part), middle)
    columns = [from_quad(middle, k) for k in range(4)]
    part = lax.all_to_all(part.reshape(8, 8, 512), "z", 0, 0, tiled=True)
    r = part.sum(0)
    columns = turned(columns, quad)
    rows = jnp.concatenate([c.T for c in columns], axis=1)
    columns = jnp.concatenate(columns, axis=0)

    r0, r1 = r[:, :256], r[:, 256:]
    s = jnp.concatenate([jnp.where(mine == k, r1, 0.0) for k in range(4)], axis=1) - exact(r0, rows, ((1,), (0,)))
    core, xh = lax.axis_index("core"), lax.axis_index("xh")
    sent = jnp.concatenate([r0, s], axis=1)
    other = near(sent)
    pair = ordered(core, sent[:, :256], other[:, :256])
    sent = jnp.concatenate([pair, sent[:, 256:] + other[:, 256:]], axis=1)
    other = opposite(sent)
    f0 = exact(ordered(xh, sent[:, :512], other[:, :512]), inverse[0], ((1,), (1,)))
    f1 = exact(sent[:, 512:] + other[:, 512:], inverse[1], ((1,), (1,)))
    b0 = exact(f0, inverse[0], ((1,), (0,)))
    b1 = exact(f1, inverse[1], ((1,), (0,)))
    other = near(jnp.concatenate([b1, block_of(b0, mine ^ 1), block_of(b0, mine ^ 3)], axis=1))
    sums = jnp.concatenate([b1, block_of(b0, mine), block_of(b0, mine ^ 2)], axis=1) + other
    other = opposite(jnp.concatenate([sums[:, :1024], sums[:, 1280:]], axis=1))
    b = sums[:, :1280] + other
    b1 = b[:, :1024]
    b0 = b[:, 1024:] - exact(b1, columns, ((1,), (0,)))
    forward = jnp.stack([f0, f1])
    backward = jnp.stack([b0, block_of(b1, mine)])
    return (forward.transpose(0, 2, 1), backward.transpose(0, 2, 1))


def solution(mesh):
    fine = Mesh(mesh.devices.reshape(8, 2, 4, 2, 2), AXES)
    placed = (P(None, COL, ROW), P(ROW, None), P(None, COL, ROW), P(None, COL, None), P(COL, None))
    return jax.shard_map(
        shards,
        mesh=fine,
        in_specs=placed,
        out_specs=(P(None, COL, ROW), P(None, COL, ROW)),
        check_vma=False,
    )
```
